256 devices in a mesh: seq: 32 (over x, z), head: 8 (over y, core).
Axes of the slice: x: 4, y: 4, z: 8, core: 2. Of those that a mesh axis runs over, the one named last changes fastest.
Arguments:
- queries: bfloat16 [32768, 5120], P('seq', 'head')
- keys: bfloat16 [32768, 5120], P('seq', 'head')
- values: bfloat16 [32768, 5120], P('seq', 'head'), may hold values from -6 to 6
- query_gain: float32 [5120], P('head'), may hold values from 0.1 to 1.9
- key_gain: float32 [5120], P('head'), may hold values from 0.1 to 1.9
- shapes: int32 [8, 3], replicated, may hold values from 4 to 32, as said below
- windows: int32 [256, 27], P('seq'), may hold values from -1 to 255, as said below
- text_keys: bfloat16 [32, 256, 5120], P(None, 'seq', 'head')
- text_values: bfloat16 [32, 256, 5120], P(None, 'seq', 'head'), may hold values from -6 to 6
- owner: int32 [8], replicated, may hold values from 0 to 31, as said below
Outputs:
- attended: bfloat16 [32768, 5120], P('seq', 'head')
The draws below stay inside these ranges and needn't reach their ends.
Inputs may be any that keep to these rules, and one draw needn't show every extreme that they name: `shapes`: row s is (frames, height, width) of video s in tokens: height and width are 16 and 32, or 32 and 16, so a frame has 4 tiles; each video has from 16 to 48 tiles, and the videos' tiles add up to 256, so no tile holds tokens of two videos. `windows`: entry k of row g stands for the tile k // 9 - 1 frames, (k // 3) % 3 - 1 tile rows and k % 3 - 1 tile columns away from tile g in its video: it holds that tile's number or -1; it is -1 wherever that tile lies outside the video, and entry 13 is always g. `owner`: no two videos share a panel.
All inputs are finite; a program needn't handle non-finite values.
Results may differ from the reference program's by a relative error of at most 0.012.
Values may be sent and summed in bfloat16 or wider, within the bound.
A program may use at most 128 MiB of HBM per device.

```python
import jax
import jax.numpy as jnp
from jax import lax

HEAD_DIM = 128
HEADS = 40
D = 5120
TILE_H = 8
TILE_W = 16
TILE = 128
WIN = 27
REACH = 7
TXT = 256
TILES_DEV = 8
TOKENS = 32768
NTILES = 256
SAMPLES = 8
PANELS = 32


def sample_shapes(key):
    half_count = SAMPLES // 2
    units = jax.random.randint(jax.random.fold_in(key, 11), (half_count,), TILES_DEV // 2, 3 * TILES_DEV // 2 + 1)
    units = units.at[0].set(3 * TILES_DEV // 2)
    partner = jax.random.permutation(jax.random.fold_in(key, 12), half_count)
    tile_counts = 4 * jnp.concatenate([units, 2 * TILES_DEV - units[partner]])
    shuffle = jax.random.permutation(jax.random.fold_in(key, 13), SAMPLES)
    tile_counts = tile_counts[shuffle]
    landscape = jax.random.randint(jax.random.fold_in(key, 14), (SAMPLES,), 0, 2) == 1
    landscape = jnp.where(tile_counts == 6 * TILES_DEV, True, jnp.where(tile_counts == 2 * TILES_DEV, False, landscape))
    row_counts = jnp.where(landscape, 2, 4)
    col_counts = jnp.where(landscape, 2, 1)
    frame_counts = tile_counts // 4
    return jnp.stack([frame_counts, row_counts * TILE_H, col_counts * TILE_W], axis=1).astype(jnp.int32)


def draw_shapes(key, part):
    return sample_shapes(key)


def draw_windows(key, part):
    shape_rows = sample_shapes(key)
    row_counts = shape_rows[:, 1] // TILE_H
    col_counts = shape_rows[:, 2] // TILE_W
    tile_counts = shape_rows[:, 0] * row_counts * col_counts
    tile_ends = jnp.cumsum(tile_counts).astype(jnp.int32)
    tile_starts = tile_ends - tile_counts
    tile_ids = jnp.arange(NTILES, dtype=jnp.int32)
    sample_ids = jnp.sum((tile_ids[:, None] >= tile_ends[None, :]).astype(jnp.int32), axis=1)
    first_tiles = tile_starts[sample_ids]
    rows_here = row_counts[sample_ids]
    cols_here = col_counts[sample_ids]
    frame_counts = shape_rows[sample_ids, 0]
    offsets = tile_ids - first_tiles
    per_frame = rows_here * cols_here
    frames = offsets // per_frame
    within = offsets % per_frame
    bands = within // cols_here
    columns = within % cols_here
    slots = jnp.arange(WIN, dtype=jnp.int32)
    time_step = slots // 9 - 1
    band_step = slots // 3 % 3 - 1
    column_step = slots % 3 - 1
    near_frame = frames[:, None] + time_step[None, :]
    near_band = bands[:, None] + band_step[None, :]
    near_column = columns[:, None] + column_step[None, :]
    inside = (near_frame >= 0) & (near_frame < frame_counts[:, None]) & (near_band >= 0) & (near_band < rows_here[:, None]) & (near_column >= 0) & (near_column < cols_here[:, None])
    chosen = jax.random.randint(jax.random.fold_in(key, 21), (NTILES, WIN), 0, 2) == 1
    chosen = chosen | ((time_step == 0) & (band_step == 0) & (column_step == 0))[None, :]
    near_ids = first_tiles[:, None] + near_frame * per_frame[:, None] + near_band * cols_here[:, None] + near_column
    return jnp.where(inside & chosen, near_ids, -1).astype(jnp.int32)


def feature_field(key):
    columns = jnp.arange(D, dtype=jnp.float32) / D
    rough = jnp.exp(jax.random.uniform(jax.random.fold_in(key, 31), (D,), minval=-0.35, maxval=0.35))
    column_scale = 3.0 ** (0.5 * columns) * rough
    row_scale = jnp.exp(jax.random.uniform(jax.random.fold_in(key, 32), (TOKENS, 1), minval=0.0, maxval=2.31))
    entries = jax.random.normal(jax.random.fold_in(key, 33), (TOKENS, D), dtype=jnp.float32)
    return entries * row_scale * column_scale[None, :]


def draw_queries(key, part):
    return feature_field(jax.random.fold_in(key, 41)).astype(jnp.bfloat16)


def draw_keys(key, part):
    return feature_field(jax.random.fold_in(key, 42)).astype(jnp.bfloat16)


def draw_text_keys(key, part):
    inner_key = jax.random.fold_in(key, 51)
    entries = jax.random.normal(inner_key, (PANELS, TXT, D), dtype=jnp.float32)
    return entries.astype(jnp.bfloat16)


def draw_owner(key, part):
    others = jax.random.permutation(jax.random.fold_in(key, 61), PANELS - 1)[:SAMPLES - 1].astype(jnp.int32)
    chosen = jnp.concatenate([others, jnp.full((1,), PANELS - 1, dtype=jnp.int32)])
    order = jax.random.permutation(jax.random.fold_in(key, 62), SAMPLES)
    return chosen[order].astype(jnp.int32)


def level_of(own_key, shape, pieces, least, high):
    level, own = 1.0, jax.random.fold_in(own_key, 6)
    for axis_at, shards_of in pieces:
        steps = jnp.exp(jax.random.uniform(jax.random.fold_in(own, axis_at), (shards_of,), jnp.float32, least / len(pieces), high / len(pieces)))
        level = level * jnp.repeat(steps, shape[axis_at] // shards_of).reshape([-1 if axis == axis_at else 1 for axis in range(len(shape))])
    return level


def noise(key, dims, deviation, reach, pieces=(), kind=jnp.bfloat16):
    drawn = deviation * jax.random.normal(key, dims, jnp.float32)
    if pieces:
        drawn = drawn * level_of(key, dims, pieces, -0.22, 0.18)
    return jnp.clip(drawn, -reach, reach).astype(kind)


def setup_inputs(seed: int = 0) -> dict:
    splits = jax.random.split(jax.random.key(seed), 11)
    return {
        "queries": draw_queries(jax.random.fold_in(splits[10], 71), 0),
        "keys": draw_keys(jax.random.fold_in(splits[10], 71), 0),
        "values": noise(splits[2], (TOKENS, D), 1.0, 6.0, ((0, 32), (1, 8))),
        "query_gain": jnp.clip(1.0 + 0.18 * jax.random.normal(splits[3], (D,), jnp.float32), 0.1, 1.9),
        "key_gain": jnp.clip(1.0 + 0.18 * jax.random.normal(splits[4], (D,), jnp.float32), 0.1, 1.9),
        "shapes": draw_shapes(jax.random.fold_in(splits[10], 71), 0),
        "windows": draw_windows(jax.random.fold_in(splits[10], 71), 0),
        "text_keys": draw_text_keys(jax.random.fold_in(splits[10], 71), 0),
        "text_values": noise(splits[8], (PANELS, TXT, D), 1.0, 6.0, ((1, 32), (2, 8))),
        "owner": draw_owner(jax.random.fold_in(splits[10], 71), 0),
    }


epsilon = 1e-06

def tile_table(shape_rows):
    per_frame = shape_rows[:, 1] // TILE_H * (shape_rows[:, 2] // TILE_W)
    tile_counts = shape_rows[:, 0] * per_frame
    tile_ends = jnp.cumsum(tile_counts).astype(jnp.int32)
    return ((tile_ends - tile_counts).astype(jnp.int32), tile_ends)

def locate(tile_ids, shape_rows, tile_starts, tile_ends):
    sample_ids = lax.optimization_barrier(jnp.sum((tile_ids[:, None] >= tile_ends[None, :]).astype(jnp.int32), axis=1)).astype(jnp.int32)
    one_hot = (sample_ids[:, None] == jnp.arange(tile_ends.shape[0], dtype=jnp.int32)[None, :]).astype(jnp.int32)
    first_tiles = lax.optimization_barrier(jnp.sum(one_hot * tile_starts[None, :], axis=1)).astype(jnp.int32)
    row_counts = lax.optimization_barrier(jnp.sum(one_hot * (shape_rows[:, 1] // TILE_H)[None, :], axis=1)).astype(jnp.int32)
    col_counts = lax.optimization_barrier(jnp.sum(one_hot * (shape_rows[:, 2] // TILE_W)[None, :], axis=1)).astype(jnp.int32)
    offsets = tile_ids - first_tiles
    per_frame = row_counts * col_counts
    within = offsets % per_frame
    return (sample_ids, one_hot, offsets // per_frame, within // col_counts, within % col_counts)

def rope_angles(frames, bands, columns, head_size):
    inner = jnp.arange(TILE_H * TILE_W, dtype=jnp.int32)
    tile_total = frames.shape[0]
    time_pos = jnp.broadcast_to(frames[:, None], (tile_total, inner.shape[0])).reshape(-1).astype(jnp.float32)
    row_pos = (bands[:, None] * TILE_H + inner[None, :] // TILE_W).reshape(-1).astype(jnp.float32)
    col_pos = (columns[:, None] * TILE_W + inner[None, :] % TILE_W).reshape(-1).astype(jnp.float32)
    third = head_size // 6
    part_sizes = (head_size - 4 * third, 2 * third, 2 * third)
    angle_parts = []
    for position, part_size in zip((time_pos, row_pos, col_pos), part_sizes):
        frequency = 10000.0 ** (-jnp.arange(0, part_size, 2, dtype=jnp.float32) / part_size)
        angle_parts.append(position[:, None] * frequency[None, :])
    return jnp.concatenate(angle_parts, axis=1)

def rotate(field, angles):
    paired = field.reshape(field.shape[0], field.shape[1], field.shape[2] // 2, 2)
    cosine = jnp.cos(angles)[:, None, :]
    sine = jnp.sin(angles)[:, None, :]
    even_part = paired[..., 0]
    odd_part = paired[..., 1]
    turned = jnp.stack([even_part * cosine - odd_part * sine, even_part * sine + odd_part * cosine], axis=-1)
    return turned.reshape(field.shape)

def reference(queries, keys, values, query_gain, key_gain, shapes, windows, text_keys, text_values, owner):
    tile_starts, tile_ends = tile_table(shapes)
    tile_ids = jnp.arange(NTILES, dtype=jnp.int32)
    sample_ids, one_hot, frames, bands, columns = locate(tile_ids, shapes, tile_starts, tile_ends)
    panel_ids = lax.optimization_barrier(jnp.sum(one_hot * owner[None, :], axis=1)).astype(jnp.int32)

    def make_prepare(gain):

        def prepare(items):
            block_rows, frame_one, band_one, column_one = items
            angles = rope_angles(frame_one[None], band_one[None], column_one[None], HEAD_DIM)
            widened = block_rows.astype(jnp.float32)
            scaled = widened * lax.rsqrt(lax.optimization_barrier(jnp.mean(widened * widened, axis=1, keepdims=True)) + epsilon) * gain[None, :]
            return rotate(scaled.reshape(TILE, HEADS, HEAD_DIM), angles).astype(jnp.bfloat16)
        return prepare
    q_hat = lax.map(make_prepare(query_gain), (queries.reshape(NTILES, TILE, D), frames, bands, columns)).reshape(TOKENS, HEADS, HEAD_DIM)
    k_hat = lax.map(make_prepare(key_gain), (keys.reshape(NTILES, TILE, D), frames, bands, columns)).reshape(TOKENS, HEADS, HEAD_DIM)
    margin = REACH * TILE
    k_padded = jnp.pad(k_hat, ((margin, margin), (0, 0), (0, 0)))
    v_padded = jnp.pad(values.reshape(TOKENS, HEADS, HEAD_DIM), ((margin, margin), (0, 0), (0, 0)))
    span_rows = (2 * REACH + 1) * TILE
    factor = HEAD_DIM ** (-0.5)

    def attend(tile_index):
        query_rows = lax.dynamic_slice_in_dim(q_hat, tile_index * TILE, TILE, 0).astype(jnp.float32)
        key_rows = lax.dynamic_slice_in_dim(k_padded, tile_index * TILE, span_rows, 0)
        value_rows = lax.dynamic_slice_in_dim(v_padded, tile_index * TILE, span_rows, 0)
        panel = lax.dynamic_index_in_dim(panel_ids, tile_index, 0, keepdims=False)
        prompt_keys = lax.dynamic_index_in_dim(text_keys, panel, 0, keepdims=False).reshape(TXT, HEADS, HEAD_DIM)
        prompt_values = lax.dynamic_index_in_dim(text_values, panel, 0, keepdims=False).reshape(TXT, HEADS, HEAD_DIM)
        key_tiles = tile_index - REACH + jnp.arange(2 * REACH + 1, dtype=jnp.int32)
        listed = lax.dynamic_index_in_dim(windows, tile_index, 0, keepdims=False)
        allowed = jnp.any(listed[:, None] == key_tiles[None, :], axis=0) & (key_tiles >= 0)
        key_mask = jnp.concatenate([jnp.repeat(allowed, TILE), jnp.ones((TXT,), dtype=bool)])
        all_keys = jnp.concatenate([key_rows, prompt_keys], axis=0).astype(jnp.float32)
        all_values = jnp.concatenate([value_rows, prompt_values], axis=0).astype(jnp.float32)
        scores = jnp.einsum('qhd,khd->hqk', query_rows, all_keys) * factor
        scores = jnp.where(key_mask[None, None, :], scores, -jnp.inf)
        largest = lax.optimization_barrier(jnp.max(scores, axis=-1, keepdims=True))
        weights = jnp.exp(scores - largest)
        totals = lax.optimization_barrier(jnp.sum(weights, axis=-1))
        rounded = lax.optimization_barrier(weights.astype(jnp.bfloat16))
        mixed = jnp.einsum('hqk,khd->qhd', rounded.astype(jnp.float32), all_values)
        mixed = mixed / jnp.transpose(totals)[:, :, None]
        return mixed.astype(jnp.bfloat16).reshape(TILE, D)
    return lax.map(attend, tile_ids).reshape(TOKENS, D)
```

```python
import functools

import jax
import jax.numpy as jnp
import numpy as np
from jax import lax
from jax.experimental import pallas as pl
from jax.experimental.pallas import tpu as pltpu
from jax.sharding import PartitionSpec as P

HEAD_DIM = 128
D = 5120
TILE = 128
TXT = 256
SAMPLES = 8
NX, NZ = 4, 8
NSEQ = NX * NZ
NHEAD = 8
LH = 5
FRAME = 512
ROWS = 1024
WIDTH = LH * HEAD_DIM
PIECE = 8
EPSILON = 1e-06
SCALE = float(HEAD_DIM**-0.5 * np.log2(np.e))
MESH = pl.DeviceIdType.MESH
F32 = jnp.float32
BF16 = jnp.bfloat16
NEG = float("-inf")
T_ROW, R_ROW, C_ROW, TAB = 0, 16, 48, 80


def position_tables():
    third = HEAD_DIM // 6
    parts = (HEAD_DIM - 4 * third, 2 * third, 2 * third)
    counts = (16, 32, 32)
    tables = np.zeros((2, TAB, HEAD_DIM), np.float64)
    row, lane = 0, 0
    for part, count in zip(parts, counts):
        frequency = 10000.0 ** (-np.arange(0, part, 2, dtype=np.float64) / part)
        angle = np.repeat(np.arange(count)[:, None] * frequency[None, :], 2, axis=1)
        tables[0, row : row + count, lane : lane + part] = np.cos(angle)
        tables[1, row : row + count, lane : lane + part] = np.sin(angle)
        row, lane = row + count, lane + part
    return tables.astype(np.float32)


def nt(a, b):
    return lax.dot_general(a, b, (((1,), (1,)), ((), ())), preferred_element_type=F32)


def nn(a, b):
    return jnp.dot(a, b, preferred_element_type=F32)


def kernel(
    q_hbm, k_hbm, v_hbm, qg_ref, kg_ref, shapes_s, win_s, owner_s, tk_hbm, tv_hbm, tab_ref,
    out_hbm,
    qraw, kraw, vv, tkb, tvb, qh, kh, khl, vhl, gat, xs, pb, sums, coss, sins, rk, acc, ms, ls, outb, bias_s,
    loc_sem, out_sem, g_send, g_recv, v_send, v_recv, k_send, k_recv, s_send, s_recv, x_send, x_recv,
):
    me_s = lax.axis_index("seq")
    me_h = lax.axis_index("head")
    x, z = me_s // NZ, me_s % NZ

    def seq_dev(s):
        return (s, me_h)

    ring_r = seq_dev(x * NZ + (z + 1) % NZ)
    ring_l = seq_dev(x * NZ + (z + NZ - 1) % NZ)
    seq_r = seq_dev((me_s + 1) % NSEQ)
    seq_l = seq_dev((me_s + NSEQ - 1) % NSEQ)
    x_peer = [seq_dev(((x + j) % NX) * NZ + z) for j in range(1, NX)]
    h_peer = [(me_s, (me_h + j) % NHEAD) for j in range(1, NHEAD)]

    loads = [
        pltpu.make_async_copy(a, b, loc_sem.at[i])
        for i, (a, b) in enumerate(
            ((tk_hbm, tkb), (tv_hbm, tvb), (k_hbm, kraw), (q_hbm, qraw), (v_hbm, vv))
        )
    ]
    for load in loads:
        load.start()

    barrier = pltpu.get_barrier_semaphore()
    peers = [ring_r, ring_l, seq_r, seq_l] + x_peer + h_peer
    for peer in peers:
        pl.semaphore_signal(barrier, inc=1, device_id=peer, device_id_type=MESH)

    def video_of(frame):
        video, first, height, end = jnp.int32(0), jnp.int32(0), shapes_s[1, 0], jnp.int32(0)
        for s in range(SAMPLES - 1):
            count = shapes_s[0, s]
            end = end + count
            past = frame >= end
            video = video + jnp.where(past, 1, 0)
            first = first + jnp.where(past, count, 0)
            height = jnp.where(past, shapes_s[1, s + 1], height)
        return video, frame - first, height

    own_frames = []
    for f in range(2):
        _, time, height = video_of(2 * me_s + f)
        own_frames.append((time, height == 16))

    loads[0].wait()
    loads[1].wait()
    for p in range(SAMPLES):
        o = owner_s[p]
        gat[z, p, 0:PIECE, :] = tkb[o]
        gat[z, p, PIECE : 2 * PIECE, :] = tvb[o]

    pl.semaphore_wait(barrier, len(peers))

    def remote(src, dst, send, recv, dev):
        return pltpu.make_async_remote_copy(
            src_ref=src, dst_ref=dst, send_sem=send, recv_sem=recv, device_id=dev, device_id_type=MESH
        )

    def hop(i):
        right = (z + NZ - (i - 1)) % NZ
        left = (z + (i - 1)) % NZ
        half = SAMPLES // 2
        if i < 4:
            a, b = gat.at[right], gat.at[left]
        else:
            a, b = gat.at[right, pl.ds(0, half)], gat.at[left, pl.ds(half, half)]
        return (
            remote(a, a, g_send.at[0, i - 1], g_recv.at[0, i - 1], ring_r),
            remote(b, b, g_send.at[1, i - 1], g_recv.at[1, i - 1], ring_l),
        )

    hops = {}

    def start_hop(i):
        hops[i] = hop(i)
        for c in hops[i]:
            c.start()

    def end_hop(i):
        for c in hops[i]:
            c.wait_recv()

    start_hop(1)
    v_copies = [
        remote(v_hbm.at[pl.ds(FRAME, FRAME)], vhl.at[0], v_send.at[0], v_recv.at[0], seq_r),
        remote(v_hbm.at[pl.ds(0, FRAME)], vhl.at[1], v_send.at[1], v_recv.at[1], seq_l),
    ]
    for c in v_copies:
        c.start()

    eye = lax.broadcasted_iota(jnp.int32, (TILE, TILE), 0) == lax.broadcasted_iota(
        jnp.int32, (TILE, TILE), 1
    )
    loads[2].wait()
    loads[3].wait()

    def squares(j, carry):
        start = pl.multiple_of(j * TILE, TILE)
        for which, ref in ((0, qraw), (8, kraw)):
            part = jnp.zeros((TILE, HEAD_DIM), F32)
            for h in range(LH):
                w = ref[pl.ds(start, TILE), h * HEAD_DIM : (h + 1) * HEAD_DIM].astype(F32)
                part = part + w * w
            total = jnp.sum(part, axis=1, keepdims=True)
            sums[me_h, pl.ds(which + j, 1), :] = jnp.sum(
                jnp.where(eye, total, 0.0), axis=0, keepdims=True
            )
        return carry

    lax.fori_loop(0, 8, squares, 0)
    s_copies = [
        remote(sums.at[me_h], sums.at[me_h], s_send.at[j], s_recv.at[j], h_peer[j])
        for j in range(NHEAD - 1)
    ]
    for c in s_copies:
        c.start()

    times = lax.broadcasted_iota(jnp.int32, (R_ROW, HEAD_DIM), 0)
    for which, ref in ((0, coss), (1, sins)):
        for j in range(8):
            time, wide = own_frames[j // 4]
            jj = j % 4
            t_row = jnp.sum(
                jnp.where(times == time, tab_ref[which, T_ROW:R_ROW, :], 0.0), axis=0, keepdims=True
            )
            c_rows = tab_ref[which, C_ROW : C_ROW + 16, :]
            if jj % 2:
                c_rows = jnp.where(wide, tab_ref[which, C_ROW + 16 : C_ROW + 32, :], c_rows)
            short, tall = R_ROW + jj // 2 * 8, R_ROW + jj * 8
            r_rows = jnp.where(
                wide, tab_ref[which, short : short + 8, :], tab_ref[which, tall : tall + 8, :]
            )
            r_rows = r_rows + t_row
            for i in range(8):
                ref[j * TILE + i * 16 : j * TILE + (i + 1) * 16, :] = c_rows + r_rows[i : i + 1, :]

    for j in range(8):
        f, jj = j // 4, j % 4
        wide = own_frames[f][1]
        for step in range(3):
            for kk in range(4):
                slot_wide = step * 9 + (kk // 2 - jj // 2 + 1) * 3 + (kk % 2 - jj % 2 + 1)
                entry = win_s[j, slot_wide]
                if abs(kk - jj) <= 1:
                    tall = win_s[j, step * 9 + (kk - jj + 1) * 3 + 1]
                else:
                    tall = jnp.int32(-1)
                entry = jnp.where(wide, entry, tall)
                bias_s[j, (f + step) * 4 + kk] = jnp.where(entry >= 0, F32(0.0), F32(NEG))

    end_hop(1)
    start_hop(2)

    for c in s_copies:
        c.wait_recv()
    total = sums[0]
    for i in range(1, NHEAD):
        total = total + sums[i]
    rk[...] = lax.rsqrt(total / D + EPSILON)

    lane = lax.broadcasted_iota(jnp.int32, (1, HEAD_DIM), 1)
    rowi = lax.broadcasted_iota(jnp.int32, (HEAD_DIM, HEAD_DIM), 0)
    coli = lax.broadcasted_iota(jnp.int32, (HEAD_DIM, HEAD_DIM), 1)
    even = coli % 2 == 0
    swap = (
        jnp.where(even & (rowi == coli + 1), -1.0, 0.0) + jnp.where((~even) & (rowi == coli - 1), 1.0, 0.0)
    ).astype(BF16)

    def rope(raw, gain_ref, which, dst):
        gains = []
        for h in range(LH):
            g = gain_ref[h * HEAD_DIM : (h + 1) * HEAD_DIM].reshape(1, HEAD_DIM)
            gs = jnp.where(
                lane % 2 == 0, pltpu.roll(g, HEAD_DIM - 1, 1), pltpu.roll(g, 1, 1)
            )
            gains.append((g, gs))

        def body(j, carry):
            start = pl.multiple_of(j * TILE, TILE)
            row = rk[pl.ds(which + j, 1), :]
            scale = jnp.sum(jnp.where(eye, row, 0.0), axis=1, keepdims=True)
            cos = coss[pl.ds(start, TILE), :] * scale
            sin = sins[pl.ds(start, TILE), :] * scale
            for h in range(LH):
                w = raw[pl.ds(start, TILE), h * HEAD_DIM : (h + 1) * HEAD_DIM]
                g, gs = gains[h]
                y = w.astype(F32) * g * cos + nn(w, swap) * gs * sin
                dst[h, pl.ds(start, TILE), :] = y.astype(BF16)
            return carry

        lax.fori_loop(0, 8, body, 0)

    rope(kraw, kg_ref, 8, kh)
    k_copies = []
    for h in range(LH):
        k_copies.append(
            (
                remote(kh.at[h, pl.ds(FRAME, FRAME)], khl.at[0, h], k_send.at[0, h], k_recv.at[0, h], seq_r),
                remote(kh.at[h, pl.ds(0, FRAME)], khl.at[1, h], k_send.at[1, h], k_recv.at[1, h], seq_l),
            )
        )
        for c in k_copies[-1]:
            c.start()
    rope(qraw, qg_ref, 0, qh)
    end_hop(2)
    start_hop(3)
    loads[4].wait()

    def columns(h):
        return pl.ds(pl.multiple_of(h * HEAD_DIM, HEAD_DIM), HEAD_DIM)

    QB = 256

    def own_block(h, b, carry):
        start = pl.multiple_of(b * QB, QB)
        s = nt(qh[h, pl.ds(start, QB), :], kh[h])
        v = vv[:, columns(h)]
        parts = []
        for a in range(QB // TILE):
            j = b * (QB // TILE) + a
            sub = [
                s[a * TILE : (a + 1) * TILE, k * TILE : (k + 1) * TILE] + bias_s[j, 4 + k]
                for k in range(8)
            ]
            m = functools.reduce(jnp.maximum, sub)
            m = jnp.broadcast_to(jnp.max(m, axis=1, keepdims=True), (TILE, TILE))
            p = [jnp.exp2((t - m) * SCALE) for t in sub]
            rows = pl.ds(pl.multiple_of(start + a * TILE, TILE), TILE)
            ms[h, rows, :] = m
            ls[h, rows, :] = functools.reduce(jnp.add, p)
            parts.append(jnp.concatenate([t.astype(BF16) for t in p], axis=1))
        acc[h, pl.ds(start, QB), :] = nn(jnp.concatenate(parts, axis=0), v)
        return carry

    def own_head(h):
        lax.fori_loop(0, ROWS // QB, functools.partial(own_block, h), 0)

    def update(h, f, k, v, biased, b, finish):
        start = pl.multiple_of(f * FRAME + b * QB, QB)
        s = nt(qh[h, pl.ds(start, QB), :], k)
        n = k.shape[0] // TILE
        parts, alphas = [], []
        for a in range(QB // TILE):
            j = f * 4 + b * (QB // TILE) + a
            rows = pl.ds(pl.multiple_of(start + a * TILE, TILE), TILE)
            sub = [s[a * TILE : (a + 1) * TILE, i * TILE : (i + 1) * TILE] for i in range(n)]
            if biased is not None:
                sub = [t + bias_s[j, biased + i] for i, t in enumerate(sub)]
            old = ms[h, rows, :]
            m = jnp.max(functools.reduce(jnp.maximum, sub), axis=1, keepdims=True)
            m = jnp.maximum(old, m)
            alpha = jnp.exp2((old - m) * SCALE)
            p = [jnp.exp2((t - m) * SCALE) for t in sub]
            l = functools.reduce(jnp.add, p) + ls[h, rows, :] * alpha
            if finish:
                l = jnp.sum(l, axis=1, keepdims=True)
                parts.append(l)
            else:
                ms[h, rows, :] = m
                ls[h, rows, :] = l
            alphas.append((alpha, jnp.concatenate([t.astype(BF16) for t in p], axis=1)))
        mixed = nn(jnp.concatenate([w for _, w in alphas], axis=0), v)
        for a in range(QB // TILE):
            rows = pl.ds(pl.multiple_of(start + a * TILE, TILE), TILE)
            new = acc[h, rows, :] * alphas[a][0] + mixed[a * TILE : (a + 1) * TILE, :]
            if finish:
                outb[rows, columns(h)] = (new / parts[a]).astype(BF16)
            else:
                acc[h, rows, :] = new

    def own_loop(lo, hi):
        def body(h, carry):
            own_head(h)
            return carry

        lax.fori_loop(lo, hi, body, 0)

    own_loop(0, 1)
    end_hop(3)
    start_hop(4)
    own_loop(1, 2)
    end_hop(4)

    for j in range(NX):
        target = ((x + j) % NX) * NZ + z
        for t in range(2):
            video, _, _ = video_of(2 * target + t)
            for i in range(NZ):
                block = gat[i, video]
                if j == 0:
                    pb[0, t, i] = block
                else:
                    xs[j - 1, t, i] = block
    x_copies = [
        remote(xs.at[j - 1], pb.at[j], x_send.at[j - 1], x_recv.at[j - 1], x_peer[j - 1])
        for j in range(1, NX)
    ]
    for c in x_copies:
        c.start()

    own_loop(2, LH)

    for c in x_copies:
        c.wait_recv()

    def prompt_head(h, carry):
        for f in range(2):
            both = pb[:, f, :, :, columns(h)].reshape(NX * NZ, 2 * PIECE, HEAD_DIM).astype(F32)
            k = both[:, :PIECE, :].reshape(TXT, HEAD_DIM).astype(BF16)
            v = both[:, PIECE:, :].reshape(TXT, HEAD_DIM).astype(BF16)
            for b in range(FRAME // QB):
                update(h, f, k, v, None, b, False)
        return carry

    lax.fori_loop(0, LH, prompt_head, 0)

    for c in v_copies:
        c.wait_recv()
    outs = []
    for h in range(LH):
        for f in range(2):
            k_copies[h][f].wait_recv()
            k = khl[f, h]
            v = vhl[f, :, h * HEAD_DIM : (h + 1) * HEAD_DIM]
            for b in range(FRAME // QB):
                update(h, f, k, v, f * 12, b, True)
        cols = pl.ds(h * HEAD_DIM, HEAD_DIM)
        outs.append(pltpu.make_async_copy(outb.at[:, cols], out_hbm.at[:, cols], out_sem.at[h]))
        outs[-1].start()

    for i in hops:
        for c in hops[i]:
            c.wait_send()
    for c in v_copies + s_copies + x_copies + [c for pair in k_copies for c in pair]:
        c.wait_send()
    for c in outs:
        c.wait()


def local(
    queries, keys, values, query_gain, key_gain, shapes, windows, text_keys, text_values, owner
):
    anyspace = pl.BlockSpec(memory_space=pl.ANY)
    vmem = pl.BlockSpec(memory_space=pltpu.VMEM)
    smem = pl.BlockSpec(memory_space=pltpu.SMEM)
    dma = pltpu.SemaphoreType.DMA
    return pl.pallas_call(
        kernel,
        out_shape=jax.ShapeDtypeStruct((ROWS, WIDTH), BF16),
        in_specs=[anyspace] * 3 + [vmem] * 2 + [smem] * 3 + [anyspace] * 2 + [vmem],
        out_specs=anyspace,
        scratch_shapes=[
            pltpu.VMEM((ROWS, WIDTH), BF16),
            pltpu.VMEM((ROWS, WIDTH), BF16),
            pltpu.VMEM((ROWS, WIDTH), BF16),
            pltpu.VMEM((32, PIECE, WIDTH), BF16),
            pltpu.VMEM((32, PIECE, WIDTH), BF16),
            pltpu.VMEM((LH, ROWS, HEAD_DIM), BF16),
            pltpu.VMEM((LH, ROWS, HEAD_DIM), BF16),
            pltpu.VMEM((2, LH, FRAME, HEAD_DIM), BF16),
            pltpu.VMEM((2, FRAME, WIDTH), BF16),
            pltpu.VMEM((NZ, SAMPLES, 2 * PIECE, WIDTH), BF16),
            pltpu.VMEM((NX - 1, 2, NZ, 2 * PIECE, WIDTH), BF16),
            pltpu.VMEM((NX, 2, NZ, 2 * PIECE, WIDTH), BF16),
            pltpu.VMEM((NHEAD, 16, TILE), F32),
            pltpu.VMEM((ROWS, HEAD_DIM), F32),
            pltpu.VMEM((ROWS, HEAD_DIM), F32),
            pltpu.VMEM((16, TILE), F32),
            pltpu.VMEM((LH, ROWS, HEAD_DIM), F32),
            pltpu.VMEM((LH, ROWS, HEAD_DIM), F32),
            pltpu.VMEM((LH, ROWS, HEAD_DIM), F32),
            pltpu.VMEM((ROWS, WIDTH), BF16),
            pltpu.SMEM((8, 16), F32),
            dma((5,)),
            dma((LH,)),
            dma((2, 4)),
            dma((2, 4)),
            dma((2,)),
            dma((2,)),
            dma((2, LH)),
            dma((2, LH)),
            dma((NHEAD - 1,)),
            dma((NHEAD - 1,)),
            dma((NX - 1,)),
            dma((NX - 1,)),
        ],
        compiler_params=pltpu.CompilerParams(
            collective_id=0, has_side_effects=True, vmem_limit_bytes=56 * 1024 * 1024
        ),
    )(
        queries,
        keys,
        values,
        query_gain,
        key_gain,
        shapes.T,
        windows,
        owner,
        text_keys,
        text_values,
        jnp.asarray(position_tables()),
    )


def solution(mesh):
    placed = (
        P("seq", "head"),
        P("seq", "head"),
        P("seq", "head"),
        P("head"),
        P("head"),
        P(),
        P("seq", None),
        P(None, "seq", "head"),
        P(None, "seq", "head"),
        P(),
    )
    return jax.shard_map(
        local, mesh=mesh, in_specs=placed, out_specs=P("seq", "head"), check_vma=False
    )
```

```python
import functools

import jax
import jax.numpy as jnp
import numpy as np
from jax import lax
from jax.experimental import pallas as pl
from jax.experimental.pallas import tpu as pltpu
from jax.sharding import PartitionSpec as P

HEAD_DIM = 128
D = 5120
TILE = 128
TXT = 256
SAMPLES = 8
NX, NZ = 4, 8
NSEQ = NX * NZ
NHEAD = 8
LH = 5
FRAME = 512
ROWS = 1024
WIDTH = LH * HEAD_DIM
PIECE = 8
EPSILON = 1e-06
SCALE = float(HEAD_DIM**-0.5 * np.log2(np.e))
MESH = pl.DeviceIdType.MESH
F32 = jnp.float32
BF16 = jnp.bfloat16
NEG = float("-inf")
T_ROW, R_ROW, C_ROW, TAB = 0, 16, 48, 80


def position_tables():
    third = HEAD_DIM // 6
    parts = (HEAD_DIM - 4 * third, 2 * third, 2 * third)
    counts = (16, 32, 32)
    tables = np.zeros((2, TAB, HEAD_DIM), np.float64)
    row, lane = 0, 0
    for part, count in zip(parts, counts):
        frequency = 10000.0 ** (-np.arange(0, part, 2, dtype=np.float64) / part)
        angle = np.repeat(np.arange(count)[:, None] * frequency[None, :], 2, axis=1)
        tables[0, row : row + count, lane : lane + part] = np.cos(angle)
        tables[1, row : row + count, lane : lane + part] = np.sin(angle)
        row, lane = row + count, lane + part
    return tables.astype(np.float32)


def nt(a, b):
    return lax.dot_general(a, b, (((1,), (1,)), ((), ())), preferred_element_type=F32)


def nn(a, b):
    return jnp.dot(a, b, preferred_element_type=F32)


def kernel(
    q_hbm, k_hbm, v_hbm, qg_ref, kg_ref, shapes_s, win_s, owner_s, tk_hbm, tv_hbm, tab_ref,
    out_hbm,
    qraw, kraw, vv, tkb, tvb, qh, kh, khl, vhl, g0, r1, r2, r3, l1, l2, l3, g4, xs, pb, sums, coss, sins, rk, acc, ms, ls, outb, bias_s,
    loc_sem, out_sem, g_send, g_recv, v_send, v_recv, p_send, k_send, k_recv, s_send, s_recv, x_send, x_recv,
):
    me_s = lax.axis_index("seq")
    me_h = lax.axis_index("head")
    x, z = me_s // NZ, me_s % NZ

    def seq_dev(s):
        return (s, me_h)

    ring_r = seq_dev(x * NZ + (z + 1) % NZ)
    ring_l = seq_dev(x * NZ + (z + NZ - 1) % NZ)
    seq_r = seq_dev((me_s + 1) % NSEQ)
    seq_l = seq_dev((me_s + NSEQ - 1) % NSEQ)
    x_peer = [seq_dev(((x + j) % NX) * NZ + z) for j in range(1, NX)]
    h_peer = [(me_s, (me_h + j) % NHEAD) for j in range(1, NHEAD)]

    loads = [
        pltpu.make_async_copy(a, b, loc_sem.at[i])
        for i, (a, b) in enumerate(
            ((tk_hbm, tkb), (tv_hbm, tvb), (k_hbm, kraw), (q_hbm, qraw), (v_hbm, vv))
        )
    ]
    for load in loads:
        load.start()

    barrier = pltpu.get_barrier_semaphore()
    peers = [ring_r, ring_l, seq_r, seq_l] + x_peer + h_peer
    for peer in peers:
        pl.semaphore_signal(barrier, inc=1, device_id=peer, device_id_type=MESH)

    def video_of(frame):
        video, first, height, end = jnp.int32(0), jnp.int32(0), shapes_s[1, 0], jnp.int32(0)
        for s in range(SAMPLES - 1):
            count = shapes_s[0, s]
            end = end + count
            past = frame >= end
            video = video + jnp.where(past, 1, 0)
            first = first + jnp.where(past, count, 0)
            height = jnp.where(past, shapes_s[1, s + 1], height)
        return video, frame - first, height

    own_frames = []
    for f in range(2):
        _, time, height = video_of(2 * me_s + f)
        own_frames.append((time, height == 16))

    loads[0].wait()
    loads[1].wait()
    for p in range(SAMPLES):
        o = owner_s[p]
        g0[p, 0:PIECE, :] = tkb[o]
        g0[p, PIECE : 2 * PIECE, :] = tvb[o]

    pl.semaphore_wait(barrier, len(peers))

    def remote(src, dst, send, recv, dev):
        return pltpu.make_async_remote_copy(
            src_ref=src, dst_ref=dst, send_sem=send, recv_sem=recv, device_id=dev, device_id_type=MESH
        )

    rights, lefts = (g0, r1, r2, r3), (g0, l1, l2, l3)

    def hop(i):
        half = SAMPLES // 2
        a, b = rights[i - 1], lefts[i - 1]
        if i < 4:
            c, d = rights[i], lefts[i]
        else:
            a, b = a.at[pl.ds(0, half)], b.at[pl.ds(half, half)]
            c, d = g4.at[pl.ds(0, half)], g4.at[pl.ds(half, half)]
        return (
            remote(a, c, g_send.at[0, i - 1], g_recv.at[0, i - 1], ring_r),
            remote(b, d, g_send.at[1, i - 1], g_recv.at[1, i - 1], ring_l),
        )

    hops = {}

    def start_hop(i):
        hops[i] = hop(i)
        for c in hops[i]:
            c.start()

    def end_hop(i):
        for c in hops[i]:
            c.wait_recv()

    x_videos = [
        [video_of(2 * (((x + j) % NX) * NZ + z) + t)[0] for t in range(2)] for j in range(NX)
    ]
    x_copies = []

    def exchange(i):
        pieces = ((g0,), (r1, l1), (r2, l2), (r3, l3), (g4,))[i]
        at = (0, 1, 3, 5, 7)[i]
        for j in range(NX):
            for t in range(2):
                for n, piece in enumerate(pieces):
                    block = piece[x_videos[j][t]]
                    if j == 0:
                        pb[0, at + n, t] = block
                    else:
                        xs[j - 1, at + n, t] = block
        part = pl.ds(at, len(pieces))
        for j in range(1, NX):
            c = remote(
                xs.at[j - 1, part], pb.at[j, part], x_send.at[j - 1, i], x_recv.at[j - 1, i], x_peer[j - 1]
            )
            c.start()
            x_copies.append(c)

    start_hop(1)
    v_copies = []

    def send_v(i):
        rows = pl.ds(i * TILE, TILE)
        for side, first, end, dev, via in (
            (0, FRAME, NZ - 1, ring_r, x_peer[0]),
            (1, 0, 0, ring_l, x_peer[NX - 2]),
        ):
            slot = jnp.where(z == end, 1, 0)
            c = remote(
                v_hbm.at[pl.ds(first + i * TILE, TILE)],
                vhl.at[side, slot, rows],
                v_send.at[side, i],
                v_recv.at[side, slot, i],
                seq_dev(jnp.where(z == end, via[0], dev[0])),
            )
            c.start()
            v_copies.append(c)

    def passing(side, i):
        rows = pl.ds(i * TILE, TILE)
        dev = ring_r if side == 0 else ring_l
        return remote(
            vhl.at[side, 1, rows], vhl.at[side, 0, rows], p_send.at[side, i], v_recv.at[side, 0, i], dev
        )

    def pass_v(i):
        for side, start in ((0, NZ - 1), (1, 0)):

            @pl.when(z == start)
            def _():
                slot = vhl.at[side, 1, pl.ds(i * TILE, TILE)]
                remote(slot, slot, v_send.at[side, i], v_recv.at[side, 1, i], ring_r).wait_recv()
                passing(side, i).start()

    send_v(0)
    exchange(0)

    eye = lax.broadcasted_iota(jnp.int32, (TILE, TILE), 0) == lax.broadcasted_iota(
        jnp.int32, (TILE, TILE), 1
    )
    loads[2].wait()
    loads[3].wait()

    def squares(j, carry):
        start = pl.multiple_of(j * TILE, TILE)
        for which, ref in ((0, qraw), (8, kraw)):
            part = jnp.zeros((TILE, HEAD_DIM), F32)
            for h in range(LH):
                w = ref[pl.ds(start, TILE), h * HEAD_DIM : (h + 1) * HEAD_DIM].astype(F32)
                part = part + w * w
            total = jnp.sum(part, axis=1, keepdims=True)
            sums[me_h, pl.ds(which + j, 1), :] = jnp.sum(
                jnp.where(eye, total, 0.0), axis=0, keepdims=True
            )
        return carry

    lax.fori_loop(0, 8, squares, 0)
    s_copies = [
        remote(sums.at[me_h], sums.at[me_h], s_send.at[j], s_recv.at[j], h_peer[j])
        for j in range(NHEAD - 1)
    ]
    for c in s_copies:
        c.start()

    times = lax.broadcasted_iota(jnp.int32, (R_ROW, HEAD_DIM), 0)
    for which, ref in ((0, coss), (1, sins)):
        for j in range(8):
            time, wide = own_frames[j // 4]
            jj = j % 4
            t_row = jnp.sum(
                jnp.where(times == time, tab_ref[which, T_ROW:R_ROW, :], 0.0), axis=0, keepdims=True
            )
            c_rows = tab_ref[which, C_ROW : C_ROW + 16, :]
            if jj % 2:
                c_rows = jnp.where(wide, tab_ref[which, C_ROW + 16 : C_ROW + 32, :], c_rows)
            short, tall = R_ROW + jj // 2 * 8, R_ROW + jj * 8
            r_rows = jnp.where(
                wide, tab_ref[which, short : short + 8, :], tab_ref[which, tall : tall + 8, :]
            )
            r_rows = r_rows + t_row
            for i in range(8):
                ref[j * TILE + i * 16 : j * TILE + (i + 1) * 16, :] = c_rows + r_rows[i : i + 1, :]

    for j in range(8):
        f, jj = j // 4, j % 4
        wide = own_frames[f][1]
        for step in range(3):
            for kk in range(4):
                slot_wide = step * 9 + (kk // 2 - jj // 2 + 1) * 3 + (kk % 2 - jj % 2 + 1)
                entry = win_s[j, slot_wide]
                if abs(kk - jj) <= 1:
                    tall = win_s[j, step * 9 + (kk - jj + 1) * 3 + 1]
                else:
                    tall = jnp.int32(-1)
                entry = jnp.where(wide, entry, tall)
                bias_s[j, (f + step) * 4 + kk] = jnp.where(entry >= 0, F32(0.0), F32(NEG))

    end_hop(1)
    start_hop(2)
    send_v(1)
    exchange(1)

    for c in s_copies:
        c.wait_recv()
    total = sums[0]
    for i in range(1, NHEAD):
        total = total + sums[i]
    rk[...] = lax.rsqrt(total / D + EPSILON)

    lane = lax.broadcasted_iota(jnp.int32, (1, HEAD_DIM), 1)
    rowi = lax.broadcasted_iota(jnp.int32, (HEAD_DIM, HEAD_DIM), 0)
    coli = lax.broadcasted_iota(jnp.int32, (HEAD_DIM, HEAD_DIM), 1)
    even = coli % 2 == 0
    swap = (
        jnp.where(even & (rowi == coli + 1), -1.0, 0.0) + jnp.where((~even) & (rowi == coli - 1), 1.0, 0.0)
    ).astype(BF16)

    def rope(raw, gain_ref, which, dst):
        gains = []
        for h in range(LH):
            g = gain_ref[h * HEAD_DIM : (h + 1) * HEAD_DIM].reshape(1, HEAD_DIM)
            gs = jnp.where(
                lane % 2 == 0, pltpu.roll(g, HEAD_DIM - 1, 1), pltpu.roll(g, 1, 1)
            )
            gains.append((g, gs))

        def body(j, carry):
            start = pl.multiple_of(j * TILE, TILE)
            row = rk[pl.ds(which + j, 1), :]
            scale = jnp.sum(jnp.where(eye, row, 0.0), axis=1, keepdims=True)
            cos = coss[pl.ds(start, TILE), :] * scale
            sin = sins[pl.ds(start, TILE), :] * scale
            for h in range(LH):
                w = raw[pl.ds(start, TILE), h * HEAD_DIM : (h + 1) * HEAD_DIM]
                g, gs = gains[h]
                y = w.astype(F32) * g * cos + nn(w, swap) * gs * sin
                dst[h, pl.ds(start, TILE), :] = y.astype(BF16)
            return carry

        lax.fori_loop(0, 8, body, 0)

    rope(kraw, kg_ref, 8, kh)
    k_copies = []
    for h in range(LH):
        k_copies.append(
            (
                remote(kh.at[h, pl.ds(FRAME, FRAME)], khl.at[0, h], k_send.at[0, h], k_recv.at[0, h], seq_r),
                remote(kh.at[h, pl.ds(0, FRAME)], khl.at[1, h], k_send.at[1, h], k_recv.at[1, h], seq_l),
            )
        )
    rope(qraw, qg_ref, 0, qh)
    end_hop(2)
    start_hop(3)
    send_v(2)
    pass_v(0)
    exchange(2)
    loads[4].wait()

    def columns(h):
        return pl.ds(pl.multiple_of(h * HEAD_DIM, HEAD_DIM), HEAD_DIM)

    QB = 256

    def own_block(h, b, carry):
        start = pl.multiple_of(b * QB, QB)
        s = nt(qh[h, pl.ds(start, QB), :], kh[h])
        v = vv[:, columns(h)]
        parts = []
        for a in range(QB // TILE):
            j = b * (QB // TILE) + a
            sub = [
                s[a * TILE : (a + 1) * TILE, k * TILE : (k + 1) * TILE] + bias_s[j, 4 + k]
                for k in range(8)
            ]
            m = functools.reduce(jnp.maximum, sub)
            m = jnp.broadcast_to(jnp.max(m, axis=1, keepdims=True), (TILE, TILE))
            p = [jnp.exp2((t - m) * SCALE) for t in sub]
            rows = pl.ds(pl.multiple_of(start + a * TILE, TILE), TILE)
            ms[h, rows, :] = m
            ls[h, rows, :] = functools.reduce(jnp.add, p)
            parts.append(jnp.concatenate([t.astype(BF16) for t in p], axis=1))
        acc[h, pl.ds(start, QB), :] = nn(jnp.concatenate(parts, axis=0), v)
        return carry

    def own_head(h):
        lax.fori_loop(0, ROWS // QB, functools.partial(own_block, h), 0)

    def update(h, f, k, v, biased, b, finish):
        start = pl.multiple_of(f * FRAME + b * QB, QB)
        s = nt(qh[h, pl.ds(start, QB), :], k)
        n = k.shape[0] // TILE
        parts, alphas = [], []
        for a in range(QB // TILE):
            j = f * 4 + b * (QB // TILE) + a
            rows = pl.ds(pl.multiple_of(start + a * TILE, TILE), TILE)
            sub = [s[a * TILE : (a + 1) * TILE, i * TILE : (i + 1) * TILE] for i in range(n)]
            if biased is not None:
                sub = [t + bias_s[j, biased + i] for i, t in enumerate(sub)]
            old = ms[h, rows, :]
            m = jnp.max(functools.reduce(jnp.maximum, sub), axis=1, keepdims=True)
            m = jnp.maximum(old, m)
            alpha = jnp.exp2((old - m) * SCALE)
            p = [jnp.exp2((t - m) * SCALE) for t in sub]
            l = functools.reduce(jnp.add, p) + ls[h, rows, :] * alpha
            if finish:
                l = jnp.sum(l, axis=1, keepdims=True)
                parts.append(l)
            else:
                ms[h, rows, :] = m
                ls[h, rows, :] = l
            alphas.append((alpha, jnp.concatenate([t.astype(BF16) for t in p], axis=1)))
        mixed = nn(jnp.concatenate([w for _, w in alphas], axis=0), v)
        for a in range(QB // TILE):
            rows = pl.ds(pl.multiple_of(start + a * TILE, TILE), TILE)
            new = acc[h, rows, :] * alphas[a][0] + mixed[a * TILE : (a + 1) * TILE, :]
            if finish:
                outb[rows, columns(h)] = (new / parts[a]).astype(BF16)
            else:
                acc[h, rows, :] = new

    def own_loop(lo, hi):
        def body(h, carry):
            own_head(h)
            return carry

        lax.fori_loop(lo, hi, body, 0)

    own_loop(0, 1)
    end_hop(3)
    start_hop(4)
    send_v(3)
    pass_v(1)
    exchange(3)
    own_loop(1, 2)
    end_hop(4)
    exchange(4)
    pass_v(2)

    def send_k(h):
        for c in k_copies[h]:
            c.start()

    send_k(0)
    send_k(1)
    for h in range(2, LH):
        own_loop(h, h + 1)
        send_k(h)
        if h == 2:
            pass_v(3)

    for c in x_copies:
        c.wait_recv()

    def prompt_head(h, carry):
        for f in range(2):
            both = pb[:, :, f, :, columns(h)].reshape(NX * NZ, 2 * PIECE, HEAD_DIM).astype(F32)
            k = both[:, :PIECE, :].reshape(TXT, HEAD_DIM).astype(BF16)
            v = both[:, PIECE:, :].reshape(TXT, HEAD_DIM).astype(BF16)
            for b in range(FRAME // QB):
                update(h, f, k, v, None, b, False)
        return carry

    lax.fori_loop(0, LH, prompt_head, 0)

    for side in range(2):
        for i in range(4):
            rows = vhl.at[side, 0, pl.ds(i * TILE, TILE)]
            remote(rows, rows, v_send.at[side, i], v_recv.at[side, 0, i], ring_r).wait_recv()
    outs = []
    for h in range(LH):
        for f in range(2):
            k_copies[h][f].wait_recv()
            k = khl[f, h]
            v = vhl[f, 0, :, h * HEAD_DIM : (h + 1) * HEAD_DIM]
            for b in range(FRAME // QB):
                update(h, f, k, v, f * 12, b, True)
        cols = pl.ds(h * HEAD_DIM, HEAD_DIM)
        outs.append(pltpu.make_async_copy(outb.at[:, cols], out_hbm.at[:, cols], out_sem.at[h]))
        outs[-1].start()

    for i in hops:
        for c in hops[i]:
            c.wait_send()
    for side, start in ((0, NZ - 1), (1, 0)):

        @pl.when(z == start)
        def _():
            for i in range(4):
                passing(side, i).wait_send()

    for c in v_copies + s_copies + x_copies + [c for pair in k_copies for c in pair]:
        c.wait_send()
    for c in outs:
        c.wait()


def local(
    queries, keys, values, query_gain, key_gain, shapes, windows, text_keys, text_values, owner
):
    hbm = pl.BlockSpec(memory_space=pltpu.HBM)
    vmem = pl.BlockSpec(memory_space=pltpu.VMEM)
    smem = pl.BlockSpec(memory_space=pltpu.SMEM)
    dma = pltpu.SemaphoreType.DMA
    return pl.pallas_call(
        kernel,
        out_shape=jax.ShapeDtypeStruct((ROWS, WIDTH), BF16),
        in_specs=[hbm] * 3 + [vmem] * 2 + [smem] * 3 + [hbm] * 2 + [vmem],
        out_specs=pl.BlockSpec(memory_space=pl.ANY),
        scratch_shapes=[
            pltpu.VMEM((ROWS, WIDTH), BF16),
            pltpu.VMEM((ROWS, WIDTH), BF16),
            pltpu.VMEM((ROWS, WIDTH), BF16),
            pltpu.VMEM((32, PIECE, WIDTH), BF16),
            pltpu.VMEM((32, PIECE, WIDTH), BF16),
            pltpu.VMEM((LH, ROWS, HEAD_DIM), BF16),
            pltpu.VMEM((LH, ROWS, HEAD_DIM), BF16),
            pltpu.VMEM((2, LH, FRAME, HEAD_DIM), BF16),
            pltpu.VMEM((2, 2, FRAME, WIDTH), BF16),
            *[pltpu.VMEM((SAMPLES, 2 * PIECE, WIDTH), BF16)] * 8,
            pltpu.VMEM((NX - 1, NZ, 2, 2 * PIECE, WIDTH), BF16),
            pltpu.VMEM((NX, NZ, 2, 2 * PIECE, WIDTH), BF16),
            pltpu.VMEM((NHEAD, 16, TILE), F32),
            pltpu.VMEM((ROWS, HEAD_DIM), F32),
            pltpu.VMEM((ROWS, HEAD_DIM), F32),
            pltpu.VMEM((16, TILE), F32),
            pltpu.VMEM((LH, ROWS, HEAD_DIM), F32),
            pltpu.VMEM((LH, ROWS, HEAD_DIM), F32),
            pltpu.VMEM((LH, ROWS, HEAD_DIM), F32),
            pltpu.VMEM((ROWS, WIDTH), BF16),
            pltpu.SMEM((8, 16), F32),
            dma((5,)),
            dma((LH,)),
            dma((2, 4)),
            dma((2, 4)),
            dma((2, 4)),
            dma((2, 2, 4)),
            dma((2, 4)),
            dma((2, LH)),
            dma((2, LH)),
            dma((NHEAD - 1,)),
            dma((NHEAD - 1,)),
            dma((NX - 1, 5)),
            dma((NX - 1, 5)),
        ],
        compiler_params=pltpu.CompilerParams(
            collective_id=0, has_side_effects=True, vmem_limit_bytes=56 * 1024 * 1024
        ),
    )(
        queries,
        keys,
        values,
        query_gain,
        key_gain,
        shapes.T,
        windows,
        owner,
        text_keys,
        text_values,
        jnp.asarray(position_tables()),
    )


def solution(mesh):
    placed = (
        P("seq", "head"),
        P("seq", "head"),
        P("seq", "head"),
        P("head"),
        P("head"),
        P(),
        P("seq", None),
        P(None, "seq", "head"),
        P(None, "seq", "head"),
        P(),
    )
    return jax.shard_map(
        local, mesh=mesh, in_specs=placed, out_specs=P("seq", "head"), check_vma=False
    )
```

```python
import functools

import jax
import jax.numpy as jnp
import numpy as np
from jax import lax
from jax.experimental import pallas as pl
from jax.experimental.pallas import tpu as pltpu
from jax.sharding import PartitionSpec as P

HEAD_DIM = 128
D = 5120
TILE = 128
TXT = 256
SAMPLES = 8
NX, NZ = 4, 8
NSEQ = NX * NZ
NHEAD = 8
LH = 5
FRAME = 512
ROWS = 1024
WIDTH = LH * HEAD_DIM
PIECE = 8
EPSILON = 1e-06
SCALE = float(HEAD_DIM**-0.5 * np.log2(np.e))
MESH = pl.DeviceIdType.MESH
F32 = jnp.float32
BF16 = jnp.bfloat16
NEG = float("-inf")
T_ROW, R_ROW, C_ROW, TAB = 0, 16, 48, 80


def position_tables():
    third = HEAD_DIM // 6
    parts = (HEAD_DIM - 4 * third, 2 * third, 2 * third)
    counts = (16, 32, 32)
    tables = np.zeros((2, TAB, HEAD_DIM), np.float64)
    row, lane = 0, 0
    for part, count in zip(parts, counts):
        frequency = 10000.0 ** (-np.arange(0, part, 2, dtype=np.float64) / part)
        angle = np.repeat(np.arange(count)[:, None] * frequency[None, :], 2, axis=1)
        tables[0, row : row + count, lane : lane + part] = np.cos(angle)
        tables[1, row : row + count, lane : lane + part] = np.sin(angle)
        row, lane = row + count, lane + part
    return tables.astype(np.float32)


def nt(a, b):
    return lax.dot_general(a, b, (((1,), (1,)), ((), ())), preferred_element_type=F32)


def nn(a, b):
    return jnp.dot(a, b, preferred_element_type=F32)


def kernel(
    q_hbm, k_hbm, v_hbm, qg_ref, kg_ref, shapes_s, win_s, owner_s, tk_hbm, tv_hbm, tab_ref,
    out_hbm,
    qraw, kraw, vv, tkb, tvb, qh, kh, khl, vhl, g0, r1, r2, r3, l1, l2, l3, g4, xs, pb, sums, coss, sins, rk, acc, ms, ls, outb, bias_s,
    loc_sem, out_sem, g_send, g_recv, v_send, v_recv, p_send, k_send, k_recv, s_send, s_recv, x_send, x_recv,
):
    me_s = lax.axis_index("seq")
    me_h = lax.axis_index("head")
    x, z = me_s // NZ, me_s % NZ

    def seq_dev(s):
        return (s, me_h)

    ring_r = seq_dev(x * NZ + (z + 1) % NZ)
    ring_l = seq_dev(x * NZ + (z + NZ - 1) % NZ)
    seq_r = seq_dev((me_s + 1) % NSEQ)
    seq_l = seq_dev((me_s + NSEQ - 1) % NSEQ)
    x_peer = [seq_dev(((x + j) % NX) * NZ + z) for j in range(1, NX)]
    h_peer = [(me_s, (me_h + j) % NHEAD) for j in range(1, NHEAD)]

    loads = [
        pltpu.make_async_copy(a, b, loc_sem.at[i])
        for i, (a, b) in enumerate(
            ((tk_hbm, tkb), (tv_hbm, tvb), (k_hbm, kraw), (q_hbm, qraw), (v_hbm, vv))
        )
    ]
    for load in loads:
        load.start()

    barrier = pltpu.get_barrier_semaphore()
    peers = [ring_r, ring_l, seq_r, seq_l] + x_peer + h_peer
    for peer in peers:
        pl.semaphore_signal(barrier, inc=1, device_id=peer, device_id_type=MESH)

    def video_of(frame):
        video, first, height, end = jnp.int32(0), jnp.int32(0), shapes_s[1, 0], jnp.int32(0)
        for s in range(SAMPLES - 1):
            count = shapes_s[0, s]
            end = end + count
            past = frame >= end
            video = video + jnp.where(past, 1, 0)
            first = first + jnp.where(past, count, 0)
            height = jnp.where(past, shapes_s[1, s + 1], height)
        return video, frame - first, height

    own_frames = []
    for f in range(2):
        _, time, height = video_of(2 * me_s + f)
        own_frames.append((time, height == 16))

    loads[0].wait()
    loads[1].wait()
    for p in range(SAMPLES):
        o = owner_s[p]
        g0[p, 0:PIECE, :] = tkb[o]
        g0[p, PIECE : 2 * PIECE, :] = tvb[o]

    pl.semaphore_wait(barrier, len(peers))

    def remote(src, dst, send, recv, dev):
        return pltpu.make_async_remote_copy(
            src_ref=src, dst_ref=dst, send_sem=send, recv_sem=recv, device_id=dev, device_id_type=MESH
        )

    rights, lefts = (g0, r1, r2, r3), (g0, l1, l2, l3)

    def hop(i):
        half = SAMPLES // 2
        a, b = rights[i - 1], lefts[i - 1]
        if i < 4:
            c, d = rights[i], lefts[i]
        else:
            a, b = a.at[pl.ds(0, half)], b.at[pl.ds(half, half)]
            c, d = g4.at[pl.ds(0, half)], g4.at[pl.ds(half, half)]
        return (
            remote(a, c, g_send.at[0, i - 1], g_recv.at[0, i - 1], ring_r),
            remote(b, d, g_send.at[1, i - 1], g_recv.at[1, i - 1], ring_l),
        )

    hops = {}

    def start_hop(i):
        hops[i] = hop(i)
        for c in hops[i]:
            c.start()

    def end_hop(i):
        for c in hops[i]:
            c.wait_recv()

    x_videos = [
        [video_of(2 * (((x + j) % NX) * NZ + z) + t)[0] for t in range(2)] for j in range(NX)
    ]
    x_copies = []

    def exchange(i):
        pieces = ((g0,), (r1, l1), (r2, l2), (r3, l3), (g4,))[i]
        at = (0, 1, 3, 5, 7)[i]
        for j in range(NX):
            for t in range(2):
                for n, piece in enumerate(pieces):
                    block = piece[x_videos[j][t]]
                    if j == 0:
                        pb[0, at + n, t] = block
                    else:
                        xs[j - 1, at + n, t] = block
        part = pl.ds(at, len(pieces))
        for j in range(1, NX):
            c = remote(
                xs.at[j - 1, part], pb.at[j, part], x_send.at[j - 1, i], x_recv.at[j - 1, i], x_peer[j - 1]
            )
            c.start()
            x_copies.append(c)

    start_hop(1)
    v_copies = []

    def send_v(i):
        rows = pl.ds(i * TILE, TILE)
        for side, first, end, dev, via in (
            (0, FRAME, NZ - 1, ring_r, x_peer[0]),
            (1, 0, 0, ring_l, x_peer[NX - 2]),
        ):
            slot = jnp.where(z == end, 1, 0)
            c = remote(
                v_hbm.at[pl.ds(first + i * TILE, TILE)],
                vhl.at[side, slot, rows],
                v_send.at[side, i],
                v_recv.at[side, slot, i],
                seq_dev(jnp.where(z == end, via[0], dev[0])),
            )
            c.start()
            v_copies.append(c)

    def passing(side, i):
        rows = pl.ds(i * TILE, TILE)
        dev = ring_r if side == 0 else ring_l
        return remote(
            vhl.at[side, 1, rows], vhl.at[side, 0, rows], p_send.at[side, i], v_recv.at[side, 0, i], dev
        )

    def pass_v(i):
        for side, start in ((0, NZ - 1), (1, 0)):

            @pl.when(z == start)
            def _():
                slot = vhl.at[side, 1, pl.ds(i * TILE, TILE)]
                remote(slot, slot, v_send.at[side, i], v_recv.at[side, 1, i], ring_r).wait_recv()
                passing(side, i).start()

    send_v(0)
    exchange(0)

    eye = lax.broadcasted_iota(jnp.int32, (TILE, TILE), 0) == lax.broadcasted_iota(
        jnp.int32, (TILE, TILE), 1
    )
    loads[2].wait()
    loads[3].wait()

    def squares(j, carry):
        start = pl.multiple_of(j * TILE, TILE)
        for which, ref in ((0, qraw), (8, kraw)):
            part = jnp.zeros((TILE, HEAD_DIM), F32)
            for h in range(LH):
                w = ref[pl.ds(start, TILE), h * HEAD_DIM : (h + 1) * HEAD_DIM].astype(F32)
                part = part + w * w
            total = jnp.sum(part, axis=1, keepdims=True)
            sums[me_h, pl.ds(which + j, 1), :] = jnp.sum(
                jnp.where(eye, total, 0.0), axis=0, keepdims=True
            )
        return carry

    lax.fori_loop(0, 8, squares, 0)
    s_copies = [
        remote(sums.at[me_h], sums.at[me_h], s_send.at[j], s_recv.at[j], h_peer[j])
        for j in range(NHEAD - 1)
    ]
    for c in s_copies:
        c.start()

    times = lax.broadcasted_iota(jnp.int32, (R_ROW, HEAD_DIM), 0)
    for which, ref in ((0, coss), (1, sins)):
        for j in range(8):
            time, wide = own_frames[j // 4]
            jj = j % 4
            t_row = jnp.sum(
                jnp.where(times == time, tab_ref[which, T_ROW:R_ROW, :], 0.0), axis=0, keepdims=True
            )
            c_rows = tab_ref[which, C_ROW : C_ROW + 16, :]
            if jj % 2:
                c_rows = jnp.where(wide, tab_ref[which, C_ROW + 16 : C_ROW + 32, :], c_rows)
            short, tall = R_ROW + jj // 2 * 8, R_ROW + jj * 8
            r_rows = jnp.where(
                wide, tab_ref[which, short : short + 8, :], tab_ref[which, tall : tall + 8, :]
            )
            r_rows = r_rows + t_row
            for i in range(8):
                ref[j * TILE + i * 16 : j * TILE + (i + 1) * 16, :] = c_rows + r_rows[i : i + 1, :]

    for j in range(8):
        f, jj = j // 4, j % 4
        wide = own_frames[f][1]
        for step in range(3):
            for kk in range(4):
                slot_wide = step * 9 + (kk // 2 - jj // 2 + 1) * 3 + (kk % 2 - jj % 2 + 1)
                entry = win_s[j, slot_wide]
                if abs(kk - jj) <= 1:
                    tall = win_s[j, step * 9 + (kk - jj + 1) * 3 + 1]
                else:
                    tall = jnp.int32(-1)
                entry = jnp.where(wide, entry, tall)
                bias_s[j, (f + step) * 4 + kk] = jnp.where(entry >= 0, F32(0.0), F32(NEG))

    end_hop(1)
    start_hop(2)
    send_v(1)
    exchange(1)

    for c in s_copies:
        c.wait_recv()
    total = sums[0]
    for i in range(1, NHEAD):
        total = total + sums[i]
    rk[...] = lax.rsqrt(total / D + EPSILON)

    lane = lax.broadcasted_iota(jnp.int32, (1, HEAD_DIM), 1)
    rowi = lax.broadcasted_iota(jnp.int32, (HEAD_DIM, HEAD_DIM), 0)
    coli = lax.broadcasted_iota(jnp.int32, (HEAD_DIM, HEAD_DIM), 1)
    even = coli % 2 == 0
    swap = (
        jnp.where(even & (rowi == coli + 1), -1.0, 0.0) + jnp.where((~even) & (rowi == coli - 1), 1.0, 0.0)
    ).astype(BF16)

    def rope(raw, gain_ref, which, dst):
        gains = []
        for h in range(LH):
            g = gain_ref[h * HEAD_DIM : (h + 1) * HEAD_DIM].reshape(1, HEAD_DIM)
            gs = jnp.where(
                lane % 2 == 0, pltpu.roll(g, HEAD_DIM - 1, 1), pltpu.roll(g, 1, 1)
            )
            gains.append((g, gs))

        def body(j, carry):
            start = pl.multiple_of(j * TILE, TILE)
            row = rk[pl.ds(which + j, 1), :]
            scale = jnp.sum(jnp.where(eye, row, 0.0), axis=1, keepdims=True)
            cos = coss[pl.ds(start, TILE), :] * scale
            sin = sins[pl.ds(start, TILE), :] * scale
            for h in range(LH):
                w = raw[pl.ds(start, TILE), h * HEAD_DIM : (h + 1) * HEAD_DIM]
                g, gs = gains[h]
                y = w.astype(F32) * g * cos + nn(w, swap) * gs * sin
                dst[h, pl.ds(start, TILE), :] = y.astype(BF16)
            return carry

        lax.fori_loop(0, 8, body, 0)

    rope(kraw, kg_ref, 8, kh)
    k_copies = []
    for h in range(LH):
        k_copies.append(
            (
                remote(kh.at[h, pl.ds(FRAME, FRAME)], khl.at[0, h], k_send.at[0, h], k_recv.at[0, h], seq_r),
                remote(kh.at[h, pl.ds(0, FRAME)], khl.at[1, h], k_send.at[1, h], k_recv.at[1, h], seq_l),
            )
        )
    rope(qraw, qg_ref, 0, qh)
    end_hop(2)
    start_hop(3)
    send_v(2)
    pass_v(0)
    exchange(2)
    loads[4].wait()

    def columns(h):
        return pl.ds(pl.multiple_of(h * HEAD_DIM, HEAD_DIM), HEAD_DIM)

    QB = 256

    def own_block(h, b, carry):
        start = pl.multiple_of(b * QB, QB)
        s = nt(qh[h, pl.ds(start, QB), :], kh[h])
        v = vv[:, columns(h)]
        parts = []
        for a in range(QB // TILE):
            j = b * (QB // TILE) + a
            sub = [
                s[a * TILE : (a + 1) * TILE, k * TILE : (k + 1) * TILE] + bias_s[j, 4 + k]
                for k in range(8)
            ]
            m = functools.reduce(jnp.maximum, sub)
            m = jnp.broadcast_to(jnp.max(m, axis=1, keepdims=True), (TILE, TILE))
            p = [jnp.exp2((t - m) * SCALE) for t in sub]
            rows = pl.ds(pl.multiple_of(start + a * TILE, TILE), TILE)
            ms[h, rows, :] = m
            ls[h, rows, :] = functools.reduce(jnp.add, p)
            parts.append(jnp.concatenate([t.astype(BF16) for t in p], axis=1))
        acc[h, pl.ds(start, QB), :] = nn(jnp.concatenate(parts, axis=0), v)
        return carry

    def own_head(h):
        lax.fori_loop(0, ROWS // QB, functools.partial(own_block, h), 0)

    HB = 512

    def update(h, f, k, v, biased, b, finish):
        start = pl.multiple_of(f * FRAME + b * HB, HB)
        s = nt(qh[h, pl.ds(start, HB), :], k)
        n = k.shape[0] // TILE
        parts, alphas = [], []
        for a in range(HB // TILE):
            j = f * 4 + b * (HB // TILE) + a
            rows = pl.ds(pl.multiple_of(start + a * TILE, TILE), TILE)
            sub = [s[a * TILE : (a + 1) * TILE, i * TILE : (i + 1) * TILE] for i in range(n)]
            if biased is not None:
                sub = [t + bias_s[j, biased + i] for i, t in enumerate(sub)]
            old = ms[h, rows, :]
            m = jnp.max(functools.reduce(jnp.maximum, sub), axis=1, keepdims=True)
            m = jnp.maximum(old, m)
            alpha = jnp.exp2((old - m) * SCALE)
            p = [jnp.exp2((t - m) * SCALE) for t in sub]
            l = functools.reduce(jnp.add, p) + ls[h, rows, :] * alpha
            if finish:
                l = jnp.sum(l, axis=1, keepdims=True)
                parts.append(l)
            else:
                ms[h, rows, :] = m
                ls[h, rows, :] = l
            alphas.append((alpha, jnp.concatenate([t.astype(BF16) for t in p], axis=1)))
        mixed = nn(jnp.concatenate([w for _, w in alphas], axis=0), v)
        for a in range(HB // TILE):
            rows = pl.ds(pl.multiple_of(start + a * TILE, TILE), TILE)
            new = acc[h, rows, :] * alphas[a][0] + mixed[a * TILE : (a + 1) * TILE, :]
            if finish:
                outb[rows, columns(h)] = (new / parts[a]).astype(BF16)
            else:
                acc[h, rows, :] = new

    def own_loop(lo, hi):
        def body(h, carry):
            own_head(h)
            return carry

        lax.fori_loop(lo, hi, body, 0)

    own_loop(0, 1)
    end_hop(3)
    start_hop(4)
    send_v(3)
    pass_v(1)
    exchange(3)
    own_loop(1, 2)
    end_hop(4)
    exchange(4)
    pass_v(2)

    def send_k(h):
        for c in k_copies[h]:
            c.start()

    send_k(0)
    for h in range(2, LH):
        own_loop(h, h + 1)
        send_k(h - 1)
        if h == 2:
            pass_v(3)

    for c in x_copies:
        c.wait_recv()
    send_k(LH - 1)

    def prompt_head(h, carry):
        for f in range(2):
            both = pb[:, :, f, :, columns(h)].reshape(NX * NZ, 2 * PIECE, HEAD_DIM).astype(F32)
            k = both[:, :PIECE, :].reshape(TXT, HEAD_DIM).astype(BF16)
            v = both[:, PIECE:, :].reshape(TXT, HEAD_DIM).astype(BF16)
            for b in range(FRAME // HB):
                update(h, f, k, v, None, b, False)
        return carry

    lax.fori_loop(0, LH, prompt_head, 0)

    for side in range(2):
        for i in range(4):
            rows = vhl.at[side, 0, pl.ds(i * TILE, TILE)]
            remote(rows, rows, v_send.at[side, i], v_recv.at[side, 0, i], ring_r).wait_recv()
    outs = []
    for h in range(LH):
        for f in range(2):
            k_copies[h][f].wait_recv()
            k = khl[f, h]
            v = vhl[f, 0, :, h * HEAD_DIM : (h + 1) * HEAD_DIM]
            for b in range(FRAME // HB):
                update(h, f, k, v, f * 12, b, True)
        cols = pl.ds(h * HEAD_DIM, HEAD_DIM)
        outs.append(pltpu.make_async_copy(outb.at[:, cols], out_hbm.at[:, cols], out_sem.at[h]))
        outs[-1].start()

    for i in hops:
        for c in hops[i]:
            c.wait_send()
    for side, start in ((0, NZ - 1), (1, 0)):

        @pl.when(z == start)
        def _():
            for i in range(4):
                passing(side, i).wait_send()

    for c in v_copies + s_copies + x_copies + [c for pair in k_copies for c in pair]:
        c.wait_send()
    for c in outs:
        c.wait()


def local(
    queries, keys, values, query_gain, key_gain, shapes, windows, text_keys, text_values, owner
):
    hbm = pl.BlockSpec(memory_space=pltpu.HBM)
    vmem = pl.BlockSpec(memory_space=pltpu.VMEM)
    smem = pl.BlockSpec(memory_space=pltpu.SMEM)
    dma = pltpu.SemaphoreType.DMA
    return pl.pallas_call(
        kernel,
        out_shape=jax.ShapeDtypeStruct((ROWS, WIDTH), BF16),
        in_specs=[hbm] * 3 + [vmem] * 2 + [smem] * 3 + [hbm] * 2 + [vmem],
        out_specs=pl.BlockSpec(memory_space=pl.ANY),
        scratch_shapes=[
            pltpu.VMEM((ROWS, WIDTH), BF16),
            pltpu.VMEM((ROWS, WIDTH), BF16),
            pltpu.VMEM((ROWS, WIDTH), BF16),
            pltpu.VMEM((32, PIECE, WIDTH), BF16),
            pltpu.VMEM((32, PIECE, WIDTH), BF16),
            pltpu.VMEM((LH, ROWS, HEAD_DIM), BF16),
            pltpu.VMEM((LH, ROWS, HEAD_DIM), BF16),
            pltpu.VMEM((2, LH, FRAME, HEAD_DIM), BF16),
            pltpu.VMEM((2, 2, FRAME, WIDTH), BF16),
            *[pltpu.VMEM((SAMPLES, 2 * PIECE, WIDTH), BF16)] * 8,
            pltpu.VMEM((NX - 1, NZ, 2, 2 * PIECE, WIDTH), BF16),
            pltpu.VMEM((NX, NZ, 2, 2 * PIECE, WIDTH), BF16),
            pltpu.VMEM((NHEAD, 16, TILE), F32),
            pltpu.VMEM((ROWS, HEAD_DIM), F32),
            pltpu.VMEM((ROWS, HEAD_DIM), F32),
            pltpu.VMEM((16, TILE), F32),
            pltpu.VMEM((LH, ROWS, HEAD_DIM), F32),
            pltpu.VMEM((LH, ROWS, HEAD_DIM), F32),
            pltpu.VMEM((LH, ROWS, HEAD_DIM), F32),
            pltpu.VMEM((ROWS, WIDTH), BF16),
            pltpu.SMEM((8, 16), F32),
            dma((5,)),
            dma((LH,)),
            dma((2, 4)),
            dma((2, 4)),
            dma((2, 4)),
            dma((2, 2, 4)),
            dma((2, 4)),
            dma((2, LH)),
            dma((2, LH)),
            dma((NHEAD - 1,)),
            dma((NHEAD - 1,)),
            dma((NX - 1, 5)),
            dma((NX - 1, 5)),
        ],
        compiler_params=pltpu.CompilerParams(
            collective_id=0, has_side_effects=True, vmem_limit_bytes=56 * 1024 * 1024
        ),
    )(
        queries,
        keys,
        values,
        query_gain,
        key_gain,
        shapes.T,
        windows,
        owner,
        text_keys,
        text_values,
        jnp.asarray(position_tables()),
    )


def solution(mesh):
    placed = (
        P("seq", "head"),
        P("seq", "head"),
        P("seq", "head"),
        P("head"),
        P("head"),
        P(),
        P("seq", None),
        P(None, "seq", "head"),
        P(None, "seq", "head"),
        P(),
    )
    return jax.shard_map(
        local, mesh=mesh, in_specs=placed, out_specs=P("seq", "head"), check_vma=False
    )
```

```python
import functools

import jax
import jax.numpy as jnp
import numpy as np
from jax import lax
from jax.experimental import pallas as pl
from jax.experimental.pallas import tpu as pltpu
from jax.sharding import PartitionSpec as P

HEAD_DIM = 128
D = 5120
TILE = 128
TXT = 256
SAMPLES = 8
NX, NZ = 4, 8
NSEQ = NX * NZ
NHEAD = 8
LH = 5
FRAME = 512
ROWS = 1024
WIDTH = LH * HEAD_DIM
PIECE = 8
EPSILON = 1e-06
SCALE = float(HEAD_DIM**-0.5 * np.log2(np.e))
MESH = pl.DeviceIdType.MESH
F32 = jnp.float32
BF16 = jnp.bfloat16
NEG = float("-inf")
T_ROW, R_ROW, C_ROW, TAB = 0, 16, 48, 80


def position_tables():
    third = HEAD_DIM // 6
    parts = (HEAD_DIM - 4 * third, 2 * third, 2 * third)
    counts = (16, 32, 32)
    tables = np.zeros((2, TAB, HEAD_DIM), np.float64)
    row, lane = 0, 0
    for part, count in zip(parts, counts):
        frequency = 10000.0 ** (-np.arange(0, part, 2, dtype=np.float64) / part)
        angle = np.repeat(np.arange(count)[:, None] * frequency[None, :], 2, axis=1)
        tables[0, row : row + count, lane : lane + part] = np.cos(angle)
        tables[1, row : row + count, lane : lane + part] = np.sin(angle)
        row, lane = row + count, lane + part
    return tables.astype(np.float32)


def nt(a, b):
    return lax.dot_general(a, b, (((1,), (1,)), ((), ())), preferred_element_type=F32)


def nn(a, b):
    return jnp.dot(a, b, preferred_element_type=F32)


def kernel(
    q_hbm, k_hbm, v_hbm, qg_ref, kg_ref, shapes_s, win_s, owner_s, tk_hbm, tv_hbm, tab_ref,
    out_hbm,
    qraw, kraw, vv, tkb, tvb, qh, kh, khl, vhl, g0, r1, r2, r3, l1, l2, l3, g4, xs, pb, sums, coss, sins, rk, acc, ms, ls, outb, bias_s,
    loc_sem, out_sem, g_send, g_recv, v_send, v_recv, p_send, k_send, k_recv, s_send, s_recv, x_send, x_recv,
):
    me_s = lax.axis_index("seq")
    me_h = lax.axis_index("head")
    x, z = me_s // NZ, me_s % NZ

    def seq_dev(s):
        return (s, me_h)

    ring_r = seq_dev(x * NZ + (z + 1) % NZ)
    ring_l = seq_dev(x * NZ + (z + NZ - 1) % NZ)
    seq_r = seq_dev((me_s + 1) % NSEQ)
    seq_l = seq_dev((me_s + NSEQ - 1) % NSEQ)
    x_peer = [seq_dev(((x + j) % NX) * NZ + z) for j in range(1, NX)]
    h_peer = [(me_s, (me_h + j) % NHEAD) for j in range(1, NHEAD)]

    loads = [
        pltpu.make_async_copy(a, b, loc_sem.at[i])
        for i, (a, b) in enumerate(
            ((tk_hbm, tkb), (tv_hbm, tvb), (k_hbm, kraw), (q_hbm, qraw), (v_hbm, vv))
        )
    ]
    for load in loads:
        load.start()

    barrier = pltpu.get_barrier_semaphore()
    peers = [ring_r, ring_l, seq_r, seq_l] + x_peer + h_peer
    for peer in peers:
        pl.semaphore_signal(barrier, inc=1, device_id=peer, device_id_type=MESH)

    def video_of(frame):
        video, first, height, end = jnp.int32(0), jnp.int32(0), shapes_s[1, 0], jnp.int32(0)
        for s in range(SAMPLES - 1):
            count = shapes_s[0, s]
            end = end + count
            past = frame >= end
            video = video + jnp.where(past, 1, 0)
            first = first + jnp.where(past, count, 0)
            height = jnp.where(past, shapes_s[1, s + 1], height)
        return video, frame - first, height

    own_frames = []
    for f in range(2):
        _, time, height = video_of(2 * me_s + f)
        own_frames.append((time, height == 16))

    loads[0].wait()
    loads[1].wait()
    for p in range(SAMPLES):
        o = owner_s[p]
        g0[p, 0:PIECE, :] = tkb[o]
        g0[p, PIECE : 2 * PIECE, :] = tvb[o]

    pl.semaphore_wait(barrier, len(peers))

    def remote(src, dst, send, recv, dev):
        return pltpu.make_async_remote_copy(
            src_ref=src, dst_ref=dst, send_sem=send, recv_sem=recv, device_id=dev, device_id_type=MESH
        )

    rights, lefts = (g0, r1, r2, r3), (g0, l1, l2, l3)

    def hop(i):
        half = SAMPLES // 2
        a, b = rights[i - 1], lefts[i - 1]
        if i < 4:
            c, d = rights[i], lefts[i]
        else:
            a, b = a.at[pl.ds(0, half)], b.at[pl.ds(half, half)]
            c, d = g4.at[pl.ds(0, half)], g4.at[pl.ds(half, half)]
        return (
            remote(a, c, g_send.at[0, i - 1], g_recv.at[0, i - 1], ring_r),
            remote(b, d, g_send.at[1, i - 1], g_recv.at[1, i - 1], ring_l),
        )

    hops = {}

    def start_hop(i):
        hops[i] = hop(i)
        for c in hops[i]:
            c.start()

    def end_hop(i):
        for c in hops[i]:
            c.wait_recv()

    x_videos = [
        [video_of(2 * (((x + j) % NX) * NZ + z) + t)[0] for t in range(2)] for j in range(NX)
    ]
    x_copies = []

    def exchange(i):
        pieces = ((g0,), (r1, l1), (r2, l2), (r3, l3), (g4,))[i]
        at = (0, 1, 3, 5, 7)[i]
        for j in range(NX):
            for t in range(2):
                for n, piece in enumerate(pieces):
                    block = piece[x_videos[j][t]]
                    if j == 0:
                        pb[0, at + n, t] = block
                    else:
                        xs[j - 1, at + n, t] = block
        part = pl.ds(at, len(pieces))
        for j in range(1, NX):
            c = remote(
                xs.at[j - 1, part], pb.at[j, part], x_send.at[j - 1, i], x_recv.at[j - 1, i], x_peer[j - 1]
            )
            c.start()
            x_copies.append(c)

    start_hop(1)
    v_copies = []

    def send_v(i):
        rows = pl.ds(i * TILE, TILE)
        for side, first, end, dev, via in (
            (0, FRAME, NZ - 1, ring_r, x_peer[0]),
            (1, 0, 0, ring_l, x_peer[NX - 2]),
        ):
            slot = jnp.where(z == end, 1, 0)
            c = remote(
                v_hbm.at[pl.ds(first + i * TILE, TILE)],
                vhl.at[side, slot, rows],
                v_send.at[side, i],
                v_recv.at[side, slot, i],
                seq_dev(jnp.where(z == end, via[0], dev[0])),
            )
            c.start()
            v_copies.append(c)

    def passing(side, i):
        rows = pl.ds(i * TILE, TILE)
        dev = ring_r if side == 0 else ring_l
        return remote(
            vhl.at[side, 1, rows], vhl.at[side, 0, rows], p_send.at[side, i], v_recv.at[side, 0, i], dev
        )

    def pass_v(i):
        for side, start in ((0, NZ - 1), (1, 0)):

            @pl.when(z == start)
            def _():
                slot = vhl.at[side, 1, pl.ds(i * TILE, TILE)]
                remote(slot, slot, v_send.at[side, i], v_recv.at[side, 1, i], ring_r).wait_recv()
                passing(side, i).start()

    send_v(0)
    exchange(0)

    eye = lax.broadcasted_iota(jnp.int32, (TILE, TILE), 0) == lax.broadcasted_iota(
        jnp.int32, (TILE, TILE), 1
    )
    loads[2].wait()
    loads[3].wait()

    def squares(j, carry):
        start = pl.multiple_of(j * TILE, TILE)
        for which, ref in ((0, qraw), (8, kraw)):
            part = jnp.zeros((TILE, HEAD_DIM), F32)
            for h in range(LH):
                w = ref[pl.ds(start, TILE), h * HEAD_DIM : (h + 1) * HEAD_DIM].astype(F32)
                part = part + w * w
            total = jnp.sum(part, axis=1, keepdims=True)
            sums[me_h, pl.ds(which + j, 1), :] = jnp.sum(
                jnp.where(eye, total, 0.0), axis=0, keepdims=True
            )
        return carry

    lax.fori_loop(0, 8, squares, 0)
    s_copies = [
        remote(sums.at[me_h], sums.at[me_h], s_send.at[j], s_recv.at[j], h_peer[j])
        for j in range(NHEAD - 1)
    ]
    for c in s_copies:
        c.start()

    times = lax.broadcasted_iota(jnp.int32, (R_ROW, HEAD_DIM), 0)
    for which, ref in ((0, coss), (1, sins)):
        for j in range(8):
            time, wide = own_frames[j // 4]
            jj = j % 4
            t_row = jnp.sum(
                jnp.where(times == time, tab_ref[which, T_ROW:R_ROW, :], 0.0), axis=0, keepdims=True
            )
            c_rows = tab_ref[which, C_ROW : C_ROW + 16, :]
            if jj % 2:
                c_rows = jnp.where(wide, tab_ref[which, C_ROW + 16 : C_ROW + 32, :], c_rows)
            short, tall = R_ROW + jj // 2 * 8, R_ROW + jj * 8
            r_rows = jnp.where(
                wide, tab_ref[which, short : short + 8, :], tab_ref[which, tall : tall + 8, :]
            )
            r_rows = r_rows + t_row
            for i in range(8):
                ref[j * TILE + i * 16 : j * TILE + (i + 1) * 16, :] = c_rows + r_rows[i : i + 1, :]

    for j in range(8):
        f, jj = j // 4, j % 4
        wide = own_frames[f][1]
        for step in range(3):
            for kk in range(4):
                slot_wide = step * 9 + (kk // 2 - jj // 2 + 1) * 3 + (kk % 2 - jj % 2 + 1)
                entry = win_s[j, slot_wide]
                if abs(kk - jj) <= 1:
                    tall = win_s[j, step * 9 + (kk - jj + 1) * 3 + 1]
                else:
                    tall = jnp.int32(-1)
                entry = jnp.where(wide, entry, tall)
                bias_s[j, (f + step) * 4 + kk] = jnp.where(entry >= 0, F32(0.0), F32(NEG))

    end_hop(1)
    start_hop(2)
    send_v(1)
    exchange(1)

    for c in s_copies:
        c.wait_recv()
    total = sums[0]
    for i in range(1, NHEAD):
        total = total + sums[i]
    rk[...] = lax.rsqrt(total / D + EPSILON)

    lane = lax.broadcasted_iota(jnp.int32, (1, HEAD_DIM), 1)
    rowi = lax.broadcasted_iota(jnp.int32, (HEAD_DIM, HEAD_DIM), 0)
    coli = lax.broadcasted_iota(jnp.int32, (HEAD_DIM, HEAD_DIM), 1)
    even = coli % 2 == 0
    swap = (
        jnp.where(even & (rowi == coli + 1), -1.0, 0.0) + jnp.where((~even) & (rowi == coli - 1), 1.0, 0.0)
    ).astype(BF16)

    def rope(raw, gain_ref, which, dst):
        gains = []
        for h in range(LH):
            g = gain_ref[h * HEAD_DIM : (h + 1) * HEAD_DIM].reshape(1, HEAD_DIM)
            gs = jnp.where(
                lane % 2 == 0, pltpu.roll(g, HEAD_DIM - 1, 1), pltpu.roll(g, 1, 1)
            )
            gains.append((g, gs))

        def body(j, carry):
            start = pl.multiple_of(j * TILE, TILE)
            row = rk[pl.ds(which + j, 1), :]
            scale = jnp.sum(jnp.where(eye, row, 0.0), axis=1, keepdims=True)
            cos = coss[pl.ds(start, TILE), :] * scale
            sin = sins[pl.ds(start, TILE), :] * scale
            for h in range(LH):
                w = raw[pl.ds(start, TILE), h * HEAD_DIM : (h + 1) * HEAD_DIM]
                g, gs = gains[h]
                y = w.astype(F32) * g * cos + nn(w, swap) * gs * sin
                dst[h, pl.ds(start, TILE), :] = y.astype(BF16)
            return carry

        lax.fori_loop(0, 8, body, 0)

    rope(kraw, kg_ref, 8, kh)
    k_copies = []
    for h in range(LH):
        k_copies.append(
            (
                remote(kh.at[h, pl.ds(FRAME, FRAME)], khl.at[0, h], k_send.at[0, h], k_recv.at[0, h], seq_r),
                remote(kh.at[h, pl.ds(0, FRAME)], khl.at[1, h], k_send.at[1, h], k_recv.at[1, h], seq_l),
            )
        )
    end_hop(2)
    start_hop(3)
    send_v(2)
    pass_v(0)
    exchange(2)
    rope(qraw, qg_ref, 0, qh)
    loads[4].wait()

    def columns(h):
        return pl.ds(pl.multiple_of(h * HEAD_DIM, HEAD_DIM), HEAD_DIM)

    QB = 256

    def own_block(h, b, carry):
        start = pl.multiple_of(b * QB, QB)
        s = nt(qh[h, pl.ds(start, QB), :], kh[h])
        v = vv[:, columns(h)]
        parts = []
        for a in range(QB // TILE):
            j = b * (QB // TILE) + a
            sub = [
                s[a * TILE : (a + 1) * TILE, k * TILE : (k + 1) * TILE] + bias_s[j, 4 + k]
                for k in range(8)
            ]
            m = functools.reduce(jnp.maximum, sub)
            m = jnp.broadcast_to(jnp.max(m, axis=1, keepdims=True), (TILE, TILE))
            p = [jnp.exp2((t - m) * SCALE) for t in sub]
            rows = pl.ds(pl.multiple_of(start + a * TILE, TILE), TILE)
            ms[h, rows, :] = m
            ls[h, rows, :] = functools.reduce(jnp.add, p)
            parts.append(jnp.concatenate([t.astype(BF16) for t in p], axis=1))
        acc[h, pl.ds(start, QB), :] = nn(jnp.concatenate(parts, axis=0), v)
        return carry

    def own_head(h):
        lax.fori_loop(0, ROWS // QB, functools.partial(own_block, h), 0)

    HB = 512

    def update(h, f, k, v, biased, b, finish):
        start = pl.multiple_of(f * FRAME + b * HB, HB)
        s = nt(qh[h, pl.ds(start, HB), :], k)
        n = k.shape[0] // TILE
        parts, alphas = [], []
        for a in range(HB // TILE):
            j = f * 4 + b * (HB // TILE) + a
            rows = pl.ds(pl.multiple_of(start + a * TILE, TILE), TILE)
            sub = [s[a * TILE : (a + 1) * TILE, i * TILE : (i + 1) * TILE] for i in range(n)]
            if biased is not None:
                sub = [t + bias_s[j, biased + i] for i, t in enumerate(sub)]
            old = ms[h, rows, :]
            m = jnp.max(functools.reduce(jnp.maximum, sub), axis=1, keepdims=True)
            m = jnp.maximum(old, m)
            alpha = jnp.exp2((old - m) * SCALE)
            p = [jnp.exp2((t - m) * SCALE) for t in sub]
            l = functools.reduce(jnp.add, p) + ls[h, rows, :] * alpha
            if finish:
                l = jnp.sum(l, axis=1, keepdims=True)
                parts.append(l)
            else:
                ms[h, rows, :] = m
                ls[h, rows, :] = l
            alphas.append((alpha, jnp.concatenate([t.astype(BF16) for t in p], axis=1)))
        mixed = nn(jnp.concatenate([w for _, w in alphas], axis=0), v)
        for a in range(HB // TILE):
            rows = pl.ds(pl.multiple_of(start + a * TILE, TILE), TILE)
            new = acc[h, rows, :] * alphas[a][0] + mixed[a * TILE : (a + 1) * TILE, :]
            if finish:
                outb[rows, columns(h)] = (new / parts[a]).astype(BF16)
            else:
                acc[h, rows, :] = new

    def own_loop(lo, hi):
        def body(h, carry):
            own_head(h)
            return carry

        lax.fori_loop(lo, hi, body, 0)

    own_loop(0, 1)
    end_hop(3)
    start_hop(4)
    send_v(3)
    pass_v(1)
    exchange(3)
    own_loop(1, 2)
    end_hop(4)
    exchange(4)
    pass_v(2)

    def send_k(h):
        for c in k_copies[h]:
            c.start()

    send_k(0)
    for h in range(2, LH):
        own_loop(h, h + 1)
        send_k(h - 1)
        if h == 2:
            pass_v(3)

    for c in x_copies:
        c.wait_recv()
    send_k(LH - 1)

    def prompt_head(h, carry):
        for f in range(2):
            both = pb[:, :, f, :, columns(h)].reshape(NX * NZ, 2 * PIECE, HEAD_DIM).astype(F32)
            k = both[:, :PIECE, :].reshape(TXT, HEAD_DIM).astype(BF16)
            v = both[:, PIECE:, :].reshape(TXT, HEAD_DIM).astype(BF16)
            for b in range(FRAME // HB):
                update(h, f, k, v, None, b, False)
        return carry

    lax.fori_loop(0, LH, prompt_head, 0)

    for side in range(2):
        for i in range(4):
            rows = vhl.at[side, 0, pl.ds(i * TILE, TILE)]
            remote(rows, rows, v_send.at[side, i], v_recv.at[side, 0, i], ring_r).wait_recv()
    outs = []
    for h in range(LH):
        for f in range(2):
            k_copies[h][f].wait_recv()
            k = khl[f, h]
            v = vhl[f, 0, :, h * HEAD_DIM : (h + 1) * HEAD_DIM]
            for b in range(FRAME // HB):
                update(h, f, k, v, f * 12, b, True)
        cols = pl.ds(h * HEAD_DIM, HEAD_DIM)
        outs.append(pltpu.make_async_copy(outb.at[:, cols], out_hbm.at[:, cols], out_sem.at[h]))
        outs[-1].start()

    for i in hops:
        for c in hops[i]:
            c.wait_send()
    for side, start in ((0, NZ - 1), (1, 0)):

        @pl.when(z == start)
        def _():
            for i in range(4):
                passing(side, i).wait_send()

    for c in v_copies + s_copies + x_copies + [c for pair in k_copies for c in pair]:
        c.wait_send()
    for c in outs:
        c.wait()


def local(
    queries, keys, values, query_gain, key_gain, shapes, windows, text_keys, text_values, owner
):
    hbm = pl.BlockSpec(memory_space=pltpu.HBM)
    vmem = pl.BlockSpec(memory_space=pltpu.VMEM)
    smem = pl.BlockSpec(memory_space=pltpu.SMEM)
    dma = pltpu.SemaphoreType.DMA
    return pl.pallas_call(
        kernel,
        out_shape=jax.ShapeDtypeStruct((ROWS, WIDTH), BF16),
        in_specs=[hbm] * 3 + [vmem] * 2 + [smem] * 3 + [hbm] * 2 + [vmem],
        out_specs=pl.BlockSpec(memory_space=pl.ANY),
        scratch_shapes=[
            pltpu.VMEM((ROWS, WIDTH), BF16),
            pltpu.VMEM((ROWS, WIDTH), BF16),
            pltpu.VMEM((ROWS, WIDTH), BF16),
            pltpu.VMEM((32, PIECE, WIDTH), BF16),
            pltpu.VMEM((32, PIECE, WIDTH), BF16),
            pltpu.VMEM((LH, ROWS, HEAD_DIM), BF16),
            pltpu.VMEM((LH, ROWS, HEAD_DIM), BF16),
            pltpu.VMEM((2, LH, FRAME, HEAD_DIM), BF16),
            pltpu.VMEM((2, 2, FRAME, WIDTH), BF16),
            *[pltpu.VMEM((SAMPLES, 2 * PIECE, WIDTH), BF16)] * 8,
            pltpu.VMEM((NX - 1, NZ, 2, 2 * PIECE, WIDTH), BF16),
            pltpu.VMEM((NX, NZ, 2, 2 * PIECE, WIDTH), BF16),
            pltpu.VMEM((NHEAD, 16, TILE), F32),
            pltpu.VMEM((ROWS, HEAD_DIM), F32),
            pltpu.VMEM((ROWS, HEAD_DIM), F32),
            pltpu.VMEM((16, TILE), F32),
            pltpu.VMEM((LH, ROWS, HEAD_DIM), F32),
            pltpu.VMEM((LH, ROWS, HEAD_DIM), F32),
            pltpu.VMEM((LH, ROWS, HEAD_DIM), F32),
            pltpu.VMEM((ROWS, WIDTH), BF16),
            pltpu.SMEM((8, 16), F32),
            dma((5,)),
            dma((LH,)),
            dma((2, 4)),
            dma((2, 4)),
            dma((2, 4)),
            dma((2, 2, 4)),
            dma((2, 4)),
            dma((2, LH)),
            dma((2, LH)),
            dma((NHEAD - 1,)),
            dma((NHEAD - 1,)),
            dma((NX - 1, 5)),
            dma((NX - 1, 5)),
        ],
        compiler_params=pltpu.CompilerParams(
            collective_id=0, has_side_effects=True, vmem_limit_bytes=56 * 1024 * 1024
        ),
    )(
        queries,
        keys,
        values,
        query_gain,
        key_gain,
        shapes.T,
        windows,
        owner,
        text_keys,
        text_values,
        jnp.asarray(position_tables()),
    )


def solution(mesh):
    placed = (
        P("seq", "head"),
        P("seq", "head"),
        P("seq", "head"),
        P("head"),
        P("head"),
        P(),
        P("seq", None),
        P(None, "seq", "head"),
        P(None, "seq", "head"),
        P(),
    )
    return jax.shard_map(
        local, mesh=mesh, in_specs=placed, out_specs=P("seq", "head"), check_vma=False
    )
```
